32 devices in a mesh: space: 16 (over z, y, x), sub: 2 (over core).
Axes of the slice: x: 2, y: 2, z: 4, core: 2. Of those that a mesh axis runs over, the one named last changes fastest.
Arguments:
- fields: bfloat16 [131072, 256], P(('space', 'sub')), may hold values from -6 to 6
- kriging: bfloat16 [512, 256, 768], P(('space', 'sub')), may hold values from -0.21875 to 0.21875
- whitening: bfloat16 [512, 256, 256], P(('space', 'sub')), may hold values from -0.375 to 0.375
- neighbours: int32 [512, 3], P(('space', 'sub')), may hold values from 0 to 511, as said below
- home: int32 [512], replicated, may hold values from 0 to 511, as said below
Outputs:
- gradient: bfloat16 [131072, 256], P(('space', 'sub'))
The draws below stay inside these ranges and needn't reach their ends.
Inputs may be any that keep to these rules, and one draw needn't show every extreme that they name: `home`: A permutation of the slots that maps the block ids of every region onto that region's own slots. `neighbours`: the 3 x 16 references of one device name different blocks, none stored on that device. Each lies in the device's own region or in the region 1 or 2 before it along space, counting cyclically. At most 20 references of one device name blocks of one earlier region, and every device has exactly 20 towards one of its two earlier regions.
All inputs are finite; a program needn't handle non-finite values.
Results may differ from the reference program's by a relative error of at most 0.006.
Values may be sent and summed in bfloat16 or wider, within the bound.
A program may use at most 128 MiB of HBM per device.

```python
import jax
import jax.numpy as jnp
from jax import lax

PTS = 256
NBR = 3
BLK_DEV = 16
FIELDS = 256
REACH = 2
CAP = 20
ORDER = 768
REGION = 32
REGIONS = 16
NBLK = 512


def region_maps(key):
    perm_keys = jax.random.split(jax.random.fold_in(key, 11), REGIONS)
    orders = jax.vmap(lambda sub_key: jax.random.permutation(sub_key, REGION))(perm_keys).astype(jnp.int32)
    bases = (jnp.arange(REGIONS, dtype=jnp.int32) * REGION)[:, None]
    home_map = (bases + orders).reshape(-1).astype(jnp.int32)
    inverse = (bases + jnp.argsort(orders, axis=1).astype(jnp.int32)).reshape(-1).astype(jnp.int32)
    return (home_map, inverse)


def draw_home(key, part):
    return region_maps(key)[0]


def draw_neighbours(key, part):
    home_map, inverse = region_maps(key)
    device_total = NBLK // BLK_DEV
    core_total = REGION // BLK_DEV
    reference_total = NBR * BLK_DEV
    device_keys = jax.random.split(jax.random.fold_in(key, 23), device_total)

    def one_device(sub_key, device):
        region_index = device // core_total
        core_index = device % core_total
        key_list = jax.random.split(sub_key, 6)
        local_count = jax.random.randint(key_list[0], (), 3 * BLK_DEV // 4, BLK_DEV + 1)
        full_step = jax.random.randint(key_list[1], (), 1, REACH + 1)
        placed = jax.random.permutation(key_list[2], reference_total).astype(jnp.int32)
        order_near = jax.random.permutation(key_list[3], REGION - BLK_DEV).astype(jnp.int32)
        order_full = jax.random.permutation(key_list[4], REGION).astype(jnp.int32)
        order_other = jax.random.permutation(key_list[5], REGION).astype(jnp.int32)
        position = jnp.arange(reference_total, dtype=jnp.int32)
        other_start = local_count + CAP
        category_step = jnp.where(position < local_count, 0, jnp.where(position < other_start, full_step, REACH + 1 - full_step))
        index_within = jnp.where(position < local_count, position, jnp.where(position < other_start, position - local_count, position - other_start))
        near_pick = order_near[jnp.clip(index_within, 0, REGION - BLK_DEV - 1)]
        near_local = jnp.where(near_pick >= core_index * BLK_DEV, near_pick + BLK_DEV, near_pick)
        far_index = jnp.clip(index_within, 0, REGION - 1)
        far_pick = jnp.where(position < other_start, order_full[far_index], order_other[far_index])
        local_slot = jnp.where(category_step == 0, near_local, far_pick)
        region_of = (region_index - category_step) % REGIONS
        slot_value = region_of * REGION + local_slot
        block_ids = inverse[slot_value]
        return block_ids[jnp.argsort(placed)].astype(jnp.int32)
    table = jax.vmap(one_device)(device_keys, jnp.arange(device_total, dtype=jnp.int32))
    return table.reshape(NBLK, NBR).astype(jnp.int32)


def level_of(rng, dims, shards, smallest, top_value):
    def one(dim, blocks):
        draws = jax.random.uniform(jax.random.fold_in(jax.random.fold_in(rng, 6), dim), (blocks,), jnp.float32, smallest / len(shards), top_value / len(shards))
        return jnp.repeat(jnp.exp(draws), dims[dim] // blocks).reshape((-1,) + (1,) * (len(dims) - dim - 1))

    loudness = one(*shards[0])
    for cut in shards[1:]:
        loudness = loudness * one(*cut)
    return loudness


def scatter_about(own_key, dims, width, limit, cuts=(), kind=jnp.bfloat16):
    factor_of = level_of(own_key, dims, cuts, -0.22, 0.18) if cuts else 1.0
    array = jax.random.normal(own_key, dims, jnp.float32) * width * factor_of
    return jnp.minimum(jnp.maximum(array, -limit), limit).astype(kind)


def setup_inputs(seed: int = 0) -> dict:
    keys = jax.random.split(jax.random.key(seed), 6)
    return {
        "fields": scatter_about(keys[0], (NBLK * PTS, FIELDS), 1.0, 6.0, ((0, 32),)),
        "kriging": scatter_about(keys[1], (NBLK, PTS, ORDER), ORDER ** -0.5, 0.21875, ((0, 32),)),
        "whitening": scatter_about(keys[2], (NBLK, PTS, PTS), PTS ** -0.5, 0.375, ((0, 32),)),
        "neighbours": draw_neighbours(jax.random.fold_in(keys[5], 71), 0),
        "home": draw_home(jax.random.fold_in(keys[5], 71), 0),
    }


def reference(fields, kriging, whitening, neighbours, home):
    block_total = neighbours.shape[0]
    series = fields.shape[1]
    blocks = fields.reshape(block_total, PTS, series)
    slot_table = jnp.take(home, neighbours.reshape(-1)).reshape(block_total, NBR).astype(jnp.int32)
    group_count = block_total // BLK_DEV

    def one_group(accumulated, group):
        first_block = (group * BLK_DEV).astype(jnp.int32)
        own_fields = lax.dynamic_slice_in_dim(blocks, first_block, BLK_DEV, 0).astype(jnp.float32)
        kriging_part = lax.dynamic_slice_in_dim(kriging, first_block, BLK_DEV, 0).astype(jnp.float32)
        whitening_part = lax.dynamic_slice_in_dim(whitening, first_block, BLK_DEV, 0).astype(jnp.float32)
        slot_part = lax.dynamic_slice_in_dim(slot_table, first_block, BLK_DEV, 0).reshape(-1).astype(jnp.int32)
        neighbourhood = jnp.take(blocks, slot_part, axis=0).reshape(BLK_DEV, ORDER, series).astype(jnp.float32)
        prediction = jnp.einsum("bpk,bks->bps", kriging_part, neighbourhood)
        residual = lax.optimization_barrier((own_fields - prediction).astype(jnp.bfloat16)).astype(jnp.float32)
        whitened = jnp.einsum("bpq,bqs->bps", whitening_part, residual)
        whitened = lax.optimization_barrier(whitened.astype(jnp.bfloat16)).astype(jnp.float32)
        pulled = jnp.einsum("bqp,bqs->bps", whitening_part, whitened)
        pulled = lax.optimization_barrier(pulled.astype(jnp.bfloat16)).astype(jnp.float32)
        returned = jnp.einsum("bpk,bps->bks", kriging_part, pulled)
        returned = lax.optimization_barrier(returned.astype(jnp.bfloat16)).astype(jnp.float32)
        accumulated = accumulated.at[slot_part].add(returned.reshape(BLK_DEV * NBR, PTS, series))
        current = lax.dynamic_slice_in_dim(accumulated, first_block, BLK_DEV, 0)
        accumulated = lax.dynamic_update_slice_in_dim(accumulated, current - pulled, first_block, 0)
        return accumulated, None

    start_value = jnp.zeros((block_total, PTS, series), jnp.float32)
    result, unused = lax.scan(one_group, start_value, jnp.arange(group_count, dtype=jnp.int32))
    return result.reshape(block_total * PTS, series).astype(jnp.bfloat16)
```

```python
import functools

import jax
import jax.numpy as jnp
from jax import lax
from jax.experimental import pallas as pl
from jax.experimental.pallas import tpu as pltpu
from jax.sharding import PartitionSpec as P

MESH = pl.DeviceIdType.MESH
F32 = jnp.float32
BF16 = jnp.bfloat16
CHUNK = 1
PAIR = 2


def kernel(
    regions,
    fields, kriging, whitening, neighbours, home,
    out,
    held, krig, white, krig_t, white_t, back, pulled, swapped, landed, places, inverse,
    load_sem, near_s, near_r, far_s, far_r, own_s, own_r, pass_s, pass_r,
    swap_s, swap_r, low_s, low_r, deep_s, deep_r, out_sem,
):
    blocks, points, _ = fields.shape
    region = 2 * blocks
    width = kriging.shape[2] // points
    refs = blocks * width
    steps = blocks // CHUNK
    me = lax.axis_index("space")
    core = lax.axis_index("sub")
    other = 1 - core
    parity = lax.rem(me, 2)
    even = parity == 0
    flip = me + 1 - 2 * parity
    ahead = lax.rem(me + 2, regions)
    behind = lax.rem(me + regions - 2, regions)
    partner = (me, other)
    mine = core * blocks
    theirs = other * blocks

    def send(src, dst, ssem, rsem, device):
        return pltpu.make_async_remote_copy(
            src_ref=src, dst_ref=dst, send_sem=ssem, recv_sem=rsem, device_id=device, device_id_type=MESH
        )

    def piece(ref, base, i):
        return ref.at[pl.ds(base + i * CHUNK, CHUNK)]

    def far(i):
        return send(piece(fields, 0, i), piece(held, 2 * region + mine, i), far_s.at[i], far_r.at[i], (ahead, core))

    def near(i):
        return send(piece(fields, 0, i), piece(held, region + mine, i), near_s.at[i], near_r.at[i], (flip, core))

    def near_relay(i):
        return send(
            piece(held, 2 * region + mine, i), piece(held, region + mine, i), near_s.at[i], near_r.at[i], (flip, core)
        )

    def own(half):
        return send(fields, held.at[pl.ds(half, blocks)], own_s, own_r, partner)

    def handed(which, half, i):
        spot = piece(held, which * region + half, i)
        k = (which - 1) * steps + i
        return send(spot, spot, pass_s.at[k], pass_r.at[k], partner)

    barrier = pltpu.get_barrier_semaphore()
    for device in (partner, (flip, core), (ahead, core), (behind, core)):
        pl.semaphore_signal(barrier, inc=1, device_id=device, device_id_type=MESH)
    pl.semaphore_wait(barrier, 4)

    @pl.loop(0, steps)
    def _(i):
        far(i).start()

        @pl.when(even)
        def _():
            near(i).start()

    load_w = pltpu.make_async_copy(whitening, white, load_sem.at[0])
    load_k = pltpu.make_async_copy(kriging, krig, load_sem.at[1])
    load_f = pltpu.make_async_copy(fields, held.at[pl.ds(mine, blocks)], load_sem.at[2])
    load_w.start()
    load_k.start()
    load_f.start()
    own(mine).start()

    back[refs] = jnp.zeros((points, fields.shape[2]), BF16)

    @pl.loop(0, blocks)
    def _(b):
        for k in range(width):
            slot = home[neighbours[b, k]]
            whose = slot // region
            distance = me - whose
            distance = jnp.where(distance < 0, distance + regions, distance)
            distance = jnp.minimum(distance, 2)
            places[b * width + k] = distance * region + slot - whose * region

    load_w.wait()
    load_k.wait()
    load_f.wait()
    targets = 3 * region // steps

    @pl.loop(0, steps)
    def _(i):
        far(i).wait_recv()

        @pl.when(parity == 1)
        def _():
            near_relay(i).start()

        handed(2, mine, i).start()

        for d in range(CHUNK):
            b = i * CHUNK + d
            white_t[b] = white[b].T
            for k in range(width):
                krig_t[b * width + k] = krig[b, :, k * points : (k + 1) * points].T

        @pl.loop(0, targets)
        def _(u):
            t = i * targets + u
            found = jnp.int32(refs)
            for j in range(refs):
                found = jnp.where(places[j] == t, j, found)
            inverse[t] = found

        near(i).wait_recv()
        handed(1, mine, i).start()

    own(theirs).wait_recv()

    @pl.loop(0, steps)
    def _(i):
        handed(2, theirs, i).wait_recv()
        handed(1, theirs, i).wait_recv()

    def dot(a, b):
        return jnp.dot(a, b, preferred_element_type=F32)

    @pl.loop(0, blocks // PAIR)
    def _(g):
        group = [g * PAIR + d for d in range(PAIR)]
        preds = []
        for b in group:
            total = None
            for k in range(width):
                term = dot(krig[b, :, k * points : (k + 1) * points], held[places[b * width + k]])
                total = term if total is None else total + term
            preds.append(total)
        rests = [(held[mine + b].astype(F32) - p).astype(BF16) for b, p in zip(group, preds)]
        whites = [dot(white[b], r).astype(BF16) for b, r in zip(group, rests)]
        pulls = [dot(white_t[b], w).astype(BF16) for b, w in zip(group, whites)]
        for b, p in zip(group, pulls):
            pulled[b] = p
        for b, p in zip(group, pulls):
            for k in range(width):
                back[b * width + k] = dot(krig_t[b * width + k], p).astype(BF16)

    own(mine).wait_send()

    @pl.loop(0, steps)
    def _(i):
        far(i).wait_send()
        near(i).wait_send()
        handed(2, mine, i).wait_send()
        handed(1, mine, i).wait_send()

    def swap(which, i):
        k = which * steps + i
        return send(
            piece(held, which * blocks, i), piece(swapped, which * blocks, i), swap_s.at[k], swap_r.at[k], partner
        )

    def offer(which, i):
        for d in range(CHUNK):
            t = i * CHUNK + d
            held[which * blocks + t] = back[inverse[which * region + theirs + t]]
        swap(which, i).start()

    sums = 3 * blocks

    def low(i):
        return send(piece(held, sums, i), piece(landed, 0, i), low_s.at[i], low_r.at[i], (flip, core))

    def deep(i):
        return send(
            piece(held, sums + blocks, i), piece(landed, blocks, i), deep_s.at[i], deep_r.at[i], (behind, core)
        )

    def add_low(i):
        swap(1, i).wait_recv()
        for d in range(CHUNK):
            t = i * CHUNK + d
            total = back[inverse[region + mine + t]].astype(F32) + swapped[blocks + t].astype(F32)
            held[sums + t] = total.astype(BF16)
        low(i).start()

    def add_deep(i, relay):
        swap(2, i).wait_recv()
        if relay:
            low(i).wait_recv()
        for d in range(CHUNK):
            t = i * CHUNK + d
            total = back[inverse[2 * region + mine + t]].astype(F32) + swapped[2 * blocks + t].astype(F32)
            if relay:
                total = total + landed[t].astype(F32)
            held[sums + blocks + t] = total.astype(BF16)
        deep(i).start()

    @pl.loop(0, steps)
    def _(i):
        offer(1, i)
        offer(2, i)

    @pl.when(even)
    def _():
        @pl.loop(0, steps)
        def _(i):
            add_low(i)
            add_deep(i, False)

    @pl.when(parity == 1)
    def _():
        @pl.loop(0, steps)
        def _(i):
            add_low(i)

    @pl.loop(0, steps)
    def _(i):
        offer(0, i)

    @pl.when(parity == 1)
    def _():
        @pl.loop(0, steps)
        def _(i):
            add_deep(i, True)

    results = sums + 2 * blocks

    def store(i):
        return pltpu.make_async_copy(piece(held, results, i), piece(out, 0, i), out_sem.at[i])

    @pl.loop(0, steps)
    def _(i):
        swap(0, i).wait_recv()

        @pl.when(even)
        def _():
            low(i).wait_recv()

        deep(i).wait_recv()
        for d in range(CHUNK):
            t = i * CHUNK + d
            total = swapped[t].astype(F32) - pulled[t].astype(F32) + landed[blocks + t].astype(F32)
            total = total + jnp.where(even, landed[t].astype(F32), 0.0)
            held[results + t] = total.astype(BF16)
        store(i).start()

    @pl.loop(0, steps)
    def _(i):
        for which in range(3):
            swap(which, i).wait_send()
        low(i).wait_send()
        deep(i).wait_send()
        store(i).wait()


def body(regions, fields, kriging, whitening, neighbours, home):
    blocks, points, order = kriging.shape
    series = fields.shape[1]
    region = 2 * blocks
    refs = neighbours.size
    steps = blocks // CHUNK
    any_space = pl.BlockSpec(memory_space=pl.ANY)
    smem = pl.BlockSpec(memory_space=pltpu.SMEM)
    dma = pltpu.SemaphoreType.DMA

    def rows(count):
        return pltpu.VMEM((count, points, series), BF16)

    result = pl.pallas_call(
        functools.partial(kernel, regions),
        out_shape=jax.ShapeDtypeStruct((blocks, points, series), BF16),
        in_specs=[any_space, any_space, any_space, smem, smem],
        out_specs=any_space,
        scratch_shapes=[
            rows(3 * region),
            pltpu.VMEM((blocks, points, order), BF16),
            pltpu.VMEM((blocks, points, points), BF16),
            pltpu.VMEM((refs, points, points), BF16),
            pltpu.VMEM((blocks, points, points), BF16),
            rows(refs + 1),
            rows(blocks),
            rows(3 * blocks),
            rows(2 * blocks),
            pltpu.SMEM((refs,), jnp.int32),
            pltpu.SMEM((3 * region,), jnp.int32),
            dma((3,)),
            dma((steps,)), dma((steps,)), dma((steps,)), dma((steps,)),
            dma, dma,
            dma((2 * steps,)), dma((2 * steps,)),
            dma((3 * steps,)), dma((3 * steps,)),
            dma((steps,)), dma((steps,)), dma((steps,)), dma((steps,)),
            dma((steps,)),
        ],
        compiler_params=pltpu.CompilerParams(
            collective_id=0, has_side_effects=True, vmem_limit_bytes=56 * 1024 * 1024
        ),
        cost_estimate=pl.CostEstimate(
            flops=4 * blocks * points * series * (order + points),
            bytes_accessed=2 * (kriging.size + whitening.size + 2 * fields.size),
            transcendentals=0,
        ),
    )(fields.reshape(blocks, points, series), kriging, whitening, neighbours, home)
    return result.reshape(blocks * points, series)


def solution(mesh):
    return jax.shard_map(
        functools.partial(body, mesh.shape["space"]),
        mesh=mesh,
        in_specs=(
            P(("space", "sub"), None),
            P(("space", "sub"), None, None),
            P(("space", "sub"), None, None),
            P(("space", "sub"), None),
            P(),
        ),
        out_specs=P(("space", "sub"), None),
        check_vma=False,
    )
```

```python
import functools

import jax
import jax.numpy as jnp
from jax import lax
from jax.experimental import pallas as pl
from jax.experimental.pallas import tpu as pltpu
from jax.sharding import PartitionSpec as P

MESH = pl.DeviceIdType.MESH
F32 = jnp.float32
BF16 = jnp.bfloat16
CHUNK = 2
WINDOW = 4


def kernel(
    regions,
    fields, kriging, whitening, neighbours, home,
    out,
    held_a, held_b, krig, white, krig_t, white_t, back_a, back_b, pulled, swapped, landed, places, inverse,
    load_sem, near_s, near_r, far_s, far_r, own_s, own_r, pass_s, pass_r,
    swap_s, swap_r, low_s, low_r, deep_s, deep_r, out_sem,
):
    held = (held_a, held_b)
    swapped = (swapped.at[0], swapped.at[1])
    landed = (landed.at[0], landed.at[1])
    pulled = (pulled.at[0], pulled.at[1])
    back = (back_a, back_b)
    blocks, points, series = fields.shape
    cols = series // 2
    region = 2 * blocks
    width = kriging.shape[2] // points
    refs = blocks * width
    steps = blocks // CHUNK
    half_steps = steps // 2
    me = lax.axis_index("space")
    core = lax.axis_index("sub")
    other = 1 - core
    parity = lax.rem(me, 2)
    even = parity == 0
    odd = parity == 1
    flip = me + 1 - 2 * parity
    ahead = lax.rem(me + 2, regions)
    behind = lax.rem(me + regions - 2, regions)
    partner = (me, other)
    mine = core * blocks
    theirs = other * blocks

    def send(src, dst, ssem, rsem, device):
        return pltpu.make_async_remote_copy(
            src_ref=src, dst_ref=dst, send_sem=ssem, recv_sem=rsem, device_id=device, device_id_type=MESH
        )

    def piece(ref, h, base, i):
        return ref[h].at[pl.ds(base + i * CHUNK, CHUNK)]

    def far(h, i):
        k = h * steps + i
        return send(
            piece(held, h, mine, i), piece(held, h, 2 * region + mine, i), far_s.at[k], far_r.at[k], (ahead, core)
        )

    def near(h, i, start):
        k = h * steps + i
        return send(
            piece(held, h, start + mine, i), piece(held, h, region + mine, i),
            near_s.at[k], near_r.at[k], (flip, core),
        )

    def own(h, half):
        spot = held[h].at[pl.ds(half, blocks)]
        return send(spot, spot, own_s.at[h], own_r.at[h], partner)

    def handed(h, which, half, i):
        spot = piece(held, h, which * region + half, i)
        k = (h * 2 + which - 1) * steps + i
        return send(spot, spot, pass_s.at[k], pass_r.at[k], partner)

    def load_fields(h):
        return pltpu.make_async_copy(
            fields.at[:, :, pl.ds(h * cols, cols)], held[h].at[pl.ds(mine, blocks)], load_sem.at[2 + h]
        )

    load_w = pltpu.make_async_copy(whitening, white, load_sem.at[0])
    load_k = pltpu.make_async_copy(kriging, krig, load_sem.at[1])
    load_fields(0).start()
    load_fields(1).start()
    load_w.start()
    load_k.start()

    barrier = pltpu.get_barrier_semaphore()
    for device in (partner, (flip, core), (ahead, core), (behind, core)):
        pl.semaphore_signal(barrier, inc=1, device_id=device, device_id_type=MESH)
    pl.semaphore_wait(barrier, 4)

    def start_own(h, i):
        far(h, i).start()

        @pl.when(even)
        def _():
            near(h, i, 0).start()

    load_fields(0).wait()
    for i in range(WINDOW):
        start_own(0, i)
    own(0, mine).start()
    load_fields(1).wait()
    own(1, mine).start()

    for h in range(2):
        back[h][refs] = jnp.zeros((points, cols), BF16)

    @pl.loop(0, blocks)
    def _(b):
        for k in range(width):
            slot = home[neighbours[k, b]]
            whose = slot // region
            distance = me - whose
            distance = jnp.where(distance < 0, distance + regions, distance)
            distance = jnp.minimum(distance, 2)
            places[b * width + k] = distance * region + slot - whose * region

    load_w.wait()
    load_k.wait()
    targets = 3 * region // steps

    def relay(h, i):
        far(h, i).wait_recv()

        @pl.when(odd)
        def _():
            near(h, i, 2 * region).start()

        handed(h, 2, mine, i).start()

    def relay_near(h, i):
        near(h, i, 0).wait_recv()
        handed(h, 1, mine, i).start()

    def arrived(h):
        own(h, theirs).wait_recv()

        @pl.loop(0, steps)
        def _(i):
            handed(h, 2, theirs, i).wait_recv()
            handed(h, 1, theirs, i).wait_recv()

    def sent(h):
        own(h, mine).wait_send()

        @pl.loop(0, steps)
        def _(i):
            far(h, i).wait_send()
            near(h, i, 0).wait_send()
            handed(h, 2, mine, i).wait_send()
            handed(h, 1, mine, i).wait_send()

    def dot(a, b):
        return jnp.dot(a, b, preferred_element_type=F32)

    def compute(h, g):
        group = [g * CHUNK + d for d in range(CHUNK)]
        preds = []
        for b in group:
            total = None
            for k in range(width):
                term = dot(krig[b, :, k * points : (k + 1) * points], held[h][places[b * width + k]])
                total = term if total is None else total + term
            preds.append(total)
        rests = [(held[h][mine + b].astype(F32) - p).astype(BF16) for b, p in zip(group, preds)]
        whites = [dot(white[b], r).astype(BF16) for b, r in zip(group, rests)]
        pulls = [dot(white_t[b], w).astype(BF16) for b, w in zip(group, whites)]
        for b, p in zip(group, pulls):
            pulled[h][b] = p
        for b, p in zip(group, pulls):
            for k in range(width):
                back[h][b * width + k] = dot(krig_t[b * width + k], p).astype(BF16)

    def swap(h, which, i):
        k = (h * 3 + which) * steps + i
        return send(
            piece(held, h, which * blocks, i), piece(swapped, h, which * blocks, i),
            swap_s.at[k], swap_r.at[k], partner,
        )

    def offer(h, which, i):
        for d in range(CHUNK):
            t = i * CHUNK + d
            held[h][which * blocks + t] = back[h][inverse[which * region + theirs + t]]
        swap(h, which, i).start()

    sums = 3 * blocks
    results = sums + 2 * blocks

    def low(h, i):
        k = h * steps + i
        return send(piece(held, h, sums, i), piece(landed, h, 0, i), low_s.at[k], low_r.at[k], (flip, core))

    def deep(h, i):
        k = h * steps + i
        return send(
            piece(held, h, sums + blocks, i), piece(landed, h, blocks, i), deep_s.at[k], deep_r.at[k], (behind, core)
        )

    def add_low(h, i):
        swap(h, 1, i).wait_recv()
        for d in range(CHUNK):
            t = i * CHUNK + d
            total = back[h][inverse[region + mine + t]].astype(F32) + swapped[h][blocks + t].astype(F32)
            held[h][sums + t] = total.astype(BF16)
        low(h, i).start()

    def add_deep(h, i, relayed):
        swap(h, 2, i).wait_recv()
        if relayed:
            low(h, i).wait_recv()
        for d in range(CHUNK):
            t = i * CHUNK + d
            total = back[h][inverse[2 * region + mine + t]].astype(F32) + swapped[h][2 * blocks + t].astype(F32)
            if relayed:
                total = total + landed[h][t].astype(F32)
            held[h][sums + blocks + t] = total.astype(BF16)
        deep(h, i).start()

    def add(h, i):
        add_low(h, i)

        @pl.when(even)
        def _():
            add_deep(h, i, False)

    def return_step(h, q):
        for e in range(2):
            offer(h, 1, 2 * q + e)
            offer(h, 2, 2 * q + e)

        @pl.when(q > 0)
        def _():
            for e in range(2):
                add(h, 2 * q - 2 + e)

    def return_end(h):
        for e in range(2):
            add(h, steps - 2 + e)

    def store(h, i):
        return pltpu.make_async_copy(
            piece(held, h, results, i),
            out.at[pl.ds(i * CHUNK, CHUNK), :, pl.ds(h * cols, cols)],
            out_sem.at[h * steps + i],
        )

    def finish(h, i):
        swap(h, 0, i).wait_recv()

        @pl.when(even)
        def _():
            low(h, i).wait_recv()

        deep(h, i).wait_recv()
        for d in range(CHUNK):
            t = i * CHUNK + d
            total = swapped[h][t].astype(F32) - pulled[h][t].astype(F32) + landed[h][blocks + t].astype(F32)
            total = total + jnp.where(even, landed[h][t].astype(F32), 0.0)
            held[h][results + t] = total.astype(BF16)
        store(h, i).start()

    @pl.loop(0, steps)
    def _(i):
        @pl.when(i < steps - WINDOW)
        def _():
            start_own(0, i + WINDOW)

        @pl.when(i >= steps - WINDOW)
        def _():
            start_own(1, i + WINDOW - steps)

        relay(0, i)

        for d in range(CHUNK):
            b = i * CHUNK + d
            white_t[b] = white[b].T
            for k in range(width):
                krig_t[b * width + k] = krig[b, :, k * points : (k + 1) * points].T

        @pl.loop(0, targets)
        def _(u):
            t = i * targets + u
            found = jnp.int32(refs)
            for j in range(refs):
                found = jnp.where(places[j] == t, j, found)
            inverse[t] = found

        relay_near(0, i)

    arrived(0)

    @pl.loop(0, half_steps)
    def _(q):
        @pl.when(q < steps - WINDOW)
        def _():
            start_own(1, q + WINDOW)

        relay(1, q)
        compute(0, 2 * q)
        relay_near(1, q)
        compute(0, 2 * q + 1)

    sent(0)

    @pl.loop(0, half_steps)
    def _(q):
        @pl.when(q + half_steps < steps - WINDOW)
        def _():
            start_own(1, q + half_steps + WINDOW)

        relay(1, q + half_steps)
        return_step(0, q)
        relay_near(1, q + half_steps)

    return_end(0)
    arrived(1)

    @pl.loop(0, half_steps)
    def _(q):
        compute(1, 2 * q)
        compute(1, 2 * q + 1)

        @pl.when(odd)
        def _():
            add_deep(0, q, True)

    sent(1)

    @pl.loop(0, half_steps)
    def _(q):
        return_step(1, q)

        @pl.when(odd)
        def _():
            add_deep(0, q + half_steps, True)

    return_end(1)

    @pl.loop(0, steps)
    def _(i):
        offer(0, 0, i)
        offer(1, 0, i)

    @pl.loop(0, steps)
    def _(i):
        @pl.when(odd)
        def _():
            add_deep(1, i, True)

        finish(0, i)

    @pl.loop(0, steps)
    def _(i):
        finish(1, i)

    @pl.loop(0, steps)
    def _(i):
        for h in range(2):
            for which in range(3):
                swap(h, which, i).wait_send()
            low(h, i).wait_send()
            deep(h, i).wait_send()
            store(h, i).wait()


def body(regions, fields, kriging, whitening, neighbours, home):
    blocks, points, order = kriging.shape
    series = fields.shape[1]
    region = 2 * blocks
    refs = neighbours.size
    steps = blocks // CHUNK
    any_space = pl.BlockSpec(memory_space=pl.ANY)
    smem = pl.BlockSpec(memory_space=pltpu.SMEM)
    dma = pltpu.SemaphoreType.DMA

    def rows(count):
        return pltpu.VMEM((count, points, series // 2), BF16)

    def halves(count):
        return pltpu.VMEM((2, count, points, series // 2), BF16)

    result = pl.pallas_call(
        functools.partial(kernel, regions),
        out_shape=jax.ShapeDtypeStruct((blocks, points, series), BF16),
        in_specs=[any_space, any_space, any_space, smem, smem],
        out_specs=any_space,
        scratch_shapes=[
            rows(3 * region), rows(3 * region),
            pltpu.VMEM((blocks, points, order), BF16),
            pltpu.VMEM((blocks, points, points), BF16),
            pltpu.VMEM((refs, points, points), BF16),
            pltpu.VMEM((blocks, points, points), BF16),
            rows(refs + 1), rows(refs + 1),
            halves(blocks),
            halves(3 * blocks),
            halves(2 * blocks),
            pltpu.SMEM((refs,), jnp.int32),
            pltpu.SMEM((3 * region,), jnp.int32),
            dma((4,)),
            dma((2 * steps,)), dma((2 * steps,)), dma((2 * steps,)), dma((2 * steps,)),
            dma((2,)), dma((2,)),
            dma((4 * steps,)), dma((4 * steps,)),
            dma((6 * steps,)), dma((6 * steps,)),
            dma((2 * steps,)), dma((2 * steps,)), dma((2 * steps,)), dma((2 * steps,)),
            dma((2 * steps,)),
        ],
        compiler_params=pltpu.CompilerParams(
            collective_id=0, has_side_effects=True, vmem_limit_bytes=56 * 1024 * 1024
        ),
        cost_estimate=pl.CostEstimate(
            flops=4 * blocks * points * series * (order + points),
            bytes_accessed=2 * (kriging.size + whitening.size + 2 * fields.size),
            transcendentals=0,
        ),
    )(fields.reshape(blocks, points, series), kriging, whitening, neighbours.T, home)
    return result.reshape(blocks * points, series)


def solution(mesh):
    return jax.shard_map(
        functools.partial(body, mesh.shape["space"]),
        mesh=mesh,
        in_specs=(
            P(("space", "sub"), None),
            P(("space", "sub"), None, None),
            P(("space", "sub"), None, None),
            P(("space", "sub"), None),
            P(),
        ),
        out_specs=P(("space", "sub"), None),
        check_vma=False,
    )
```

```python
import functools

import jax
import jax.numpy as jnp
from jax import lax
from jax.experimental import pallas as pl
from jax.experimental.pallas import tpu as pltpu
from jax.sharding import PartitionSpec as P

MESH = pl.DeviceIdType.MESH
F32 = jnp.float32
BF16 = jnp.bfloat16
CHUNK = 1
WINDOW = 8
GROUP = 2
EARLY = 2


def kernel(
    regions,
    fields, kriging, whitening, neighbours, home,
    out,
    held_a, held_b, krig, white, krig_t, white_t, back_a, back_b, pulled, swapped, landed, places, inverse,
    load_sem, near_s, near_r, far_s, far_r, own_s, own_r, pass_s, pass_r,
    swap_s, swap_r, low_s, low_r, deep_s, deep_r, out_sem,
):
    held = (held_a, held_b)
    swapped = (swapped.at[0], swapped.at[1])
    landed = (landed.at[0], landed.at[1])
    pulled = (pulled.at[0], pulled.at[1])
    back = (back_a, back_b)
    blocks, points, series = fields.shape
    cols = series // 2
    region = 2 * blocks
    width = kriging.shape[2] // points
    refs = blocks * width
    steps = blocks // CHUNK
    half_steps = steps // 2
    me = lax.axis_index("space")
    core = lax.axis_index("sub")
    other = 1 - core
    parity = lax.rem(me, 2)
    even = parity == 0
    odd = parity == 1
    flip = me + 1 - 2 * parity
    ahead = lax.rem(me + 2, regions)
    behind = lax.rem(me + regions - 2, regions)
    partner = (me, other)
    mine = core * blocks
    theirs = other * blocks

    def send(src, dst, ssem, rsem, device):
        return pltpu.make_async_remote_copy(
            src_ref=src, dst_ref=dst, send_sem=ssem, recv_sem=rsem, device_id=device, device_id_type=MESH
        )

    def piece(ref, h, base, i):
        return ref[h].at[pl.ds(base + i * CHUNK, CHUNK)]

    def far(h, i):
        k = h * steps + i
        return send(
            piece(held, h, mine, i), piece(held, h, 2 * region + mine, i), far_s.at[k], far_r.at[k], (ahead, core)
        )

    def near(h, i, start):
        k = h * steps + i
        return send(
            piece(held, h, start + mine, i), piece(held, h, region + mine, i),
            near_s.at[k], near_r.at[k], (flip, core),
        )

    def own(h, half):
        spot = held[h].at[pl.ds(half, blocks)]
        return send(spot, spot, own_s.at[h], own_r.at[h], partner)

    def handed(h, which, half, i):
        spot = piece(held, h, which * region + half, i)
        k = (h * 2 + which - 1) * steps + i
        return send(spot, spot, pass_s.at[k], pass_r.at[k], partner)

    def load_fields(h):
        return pltpu.make_async_copy(
            fields.at[:, :, pl.ds(h * cols, cols)], held[h].at[pl.ds(mine, blocks)], load_sem.at[2 + h]
        )

    load_w = pltpu.make_async_copy(whitening, white, load_sem.at[0])
    load_k = pltpu.make_async_copy(kriging, krig, load_sem.at[1])
    load_fields(0).start()
    load_fields(1).start()
    load_w.start()
    load_k.start()

    barrier = pltpu.get_barrier_semaphore()
    for device in (partner, (flip, core), (ahead, core), (behind, core)):
        pl.semaphore_signal(barrier, inc=1, device_id=device, device_id_type=MESH)
    pl.semaphore_wait(barrier, 4)

    def start_own(h, i):
        far(h, i).start()

        @pl.when(even)
        def _():
            near(h, i, 0).start()

    load_fields(0).wait()
    for i in range(WINDOW):
        start_own(0, i)
    own(0, mine).start()
    load_fields(1).wait()
    own(1, mine).start()

    for h in range(2):
        back[h][refs] = jnp.zeros((points, cols), BF16)

    @pl.loop(0, blocks)
    def _(b):
        for k in range(width):
            slot = home[neighbours[k, b]]
            whose = slot // region
            distance = me - whose
            distance = jnp.where(distance < 0, distance + regions, distance)
            distance = jnp.minimum(distance, 2)
            places[b * width + k] = distance * region + slot - whose * region

    load_w.wait()
    load_k.wait()
    targets = 3 * region // steps

    def relay(h, i):
        far(h, i).wait_recv()

        @pl.when(odd)
        def _():
            near(h, i, 2 * region).start()

        handed(h, 2, mine, i).start()

    def relay_near(h, i):
        near(h, i, 0).wait_recv()
        handed(h, 1, mine, i).start()

    def arrived(h):
        own(h, theirs).wait_recv()

        @pl.loop(0, steps)
        def _(i):
            handed(h, 2, theirs, i).wait_recv()
            handed(h, 1, theirs, i).wait_recv()

    def sent(h):
        own(h, mine).wait_send()

        @pl.loop(0, steps)
        def _(i):
            far(h, i).wait_send()
            near(h, i, 0).wait_send()
            handed(h, 2, mine, i).wait_send()
            handed(h, 1, mine, i).wait_send()

    def dot(a, b):
        return jnp.dot(a, b, preferred_element_type=F32)

    def compute(h, g):
        group = [g * GROUP + d for d in range(GROUP)]
        preds = []
        for b in group:
            total = None
            for k in range(width):
                term = dot(krig[b, :, k * points : (k + 1) * points], held[h][places[b * width + k]])
                total = term if total is None else total + term
            preds.append(total)
        rests = [(held[h][mine + b].astype(F32) - p).astype(BF16) for b, p in zip(group, preds)]
        whites = [dot(white[b], r).astype(BF16) for b, r in zip(group, rests)]
        pulls = [dot(white_t[b], w).astype(BF16) for b, w in zip(group, whites)]
        for b, p in zip(group, pulls):
            pulled[h][b] = p
        for b, p in zip(group, pulls):
            for k in range(width):
                back[h][b * width + k] = dot(krig_t[b * width + k], p).astype(BF16)

    def swap(h, which, i):
        k = (h * 3 + which) * steps + i
        return send(
            piece(held, h, which * blocks, i), piece(swapped, h, which * blocks, i),
            swap_s.at[k], swap_r.at[k], partner,
        )

    def offer(h, which, i):
        for d in range(CHUNK):
            t = i * CHUNK + d
            held[h][which * blocks + t] = back[h][inverse[which * region + theirs + t]]
        swap(h, which, i).start()

    sums = 3 * blocks
    results = sums + 2 * blocks

    def low(h, i):
        k = h * steps + i
        return send(piece(held, h, sums, i), piece(landed, h, 0, i), low_s.at[k], low_r.at[k], (flip, core))

    def deep(h, i):
        k = h * steps + i
        return send(
            piece(held, h, sums + blocks, i), piece(landed, h, blocks, i), deep_s.at[k], deep_r.at[k], (behind, core)
        )

    def add_low(h, i):
        swap(h, 1, i).wait_recv()
        for d in range(CHUNK):
            t = i * CHUNK + d
            total = back[h][inverse[region + mine + t]].astype(F32) + swapped[h][blocks + t].astype(F32)
            held[h][sums + t] = total.astype(BF16)
        low(h, i).start()

    def add_deep(h, i, relayed):
        swap(h, 2, i).wait_recv()
        if relayed:
            low(h, i).wait_recv()
        for d in range(CHUNK):
            t = i * CHUNK + d
            total = back[h][inverse[2 * region + mine + t]].astype(F32) + swapped[h][2 * blocks + t].astype(F32)
            if relayed:
                total = total + landed[h][t].astype(F32)
            held[h][sums + blocks + t] = total.astype(BF16)
        deep(h, i).start()

    def add(h, i):
        add_low(h, i)

        @pl.when(even)
        def _():
            add_deep(h, i, False)

    def return_step(h, q):
        for e in range(2):
            offer(h, 1, 2 * q + e)
            offer(h, 2, 2 * q + e)

        @pl.when(q > 0)
        def _():
            for e in range(2):
                add(h, 2 * q - 2 + e)

    def return_end(h):
        for e in range(2):
            add(h, steps - 2 + e)

    def store(h, i):
        return pltpu.make_async_copy(
            piece(held, h, results, i),
            out.at[pl.ds(i * CHUNK, CHUNK), :, pl.ds(h * cols, cols)],
            out_sem.at[h * steps + i],
        )

    def finish(h, i):
        swap(h, 0, i).wait_recv()

        @pl.when(even)
        def _():
            low(h, i).wait_recv()

        deep(h, i).wait_recv()
        for d in range(CHUNK):
            t = i * CHUNK + d
            total = swapped[h][t].astype(F32) - pulled[h][t].astype(F32) + landed[h][blocks + t].astype(F32)
            total = total + jnp.where(even, landed[h][t].astype(F32), 0.0)
            held[h][results + t] = total.astype(BF16)
        store(h, i).start()

    @pl.loop(0, steps)
    def _(i):
        @pl.when(i < steps - WINDOW)
        def _():
            start_own(0, i + WINDOW)

        @pl.when(i >= steps - WINDOW)
        def _():
            start_own(1, i + WINDOW - steps)

        relay(0, i)

        for d in range(CHUNK):
            b = i * CHUNK + d
            white_t[b] = white[b].T
            for k in range(width):
                krig_t[b * width + k] = krig[b, :, k * points : (k + 1) * points].T

        @pl.loop(0, targets)
        def _(u):
            t = i * targets + u
            found = jnp.int32(refs)
            for j in range(refs):
                found = jnp.where(places[j] == t, j, found)
            inverse[t] = found

        relay_near(0, i)

    arrived(0)

    @pl.loop(0, half_steps)
    def _(q):
        @pl.when(q < steps - WINDOW)
        def _():
            start_own(1, q + WINDOW)

        relay(1, q)
        compute(0, q)
        relay_near(1, q)

    sent(0)

    @pl.loop(0, half_steps)
    def _(q):
        @pl.when(q + half_steps < steps - WINDOW)
        def _():
            start_own(1, q + half_steps + WINDOW)

        relay(1, q + half_steps)
        return_step(0, q)
        relay_near(1, q + half_steps)

    return_end(0)

    @pl.when(odd)
    def _():
        for j in range(EARLY):
            add_deep(0, j, True)

    arrived(1)

    @pl.loop(0, half_steps)
    def _(q):
        compute(1, q)

        @pl.when(odd)
        def _():
            add_deep(0, q + EARLY, True)

    sent(1)

    @pl.loop(0, half_steps)
    def _(q):
        return_step(1, q)

    return_end(1)

    @pl.when(odd)
    def _():
        @pl.loop(half_steps + EARLY, steps)
        def _(i):
            add_deep(0, i, True)

    @pl.loop(0, steps)
    def _(i):
        offer(0, 0, i)
        offer(1, 0, i)

    @pl.loop(0, steps)
    def _(i):
        @pl.when(odd)
        def _():
            add_deep(1, i, True)

        finish(0, i)

    @pl.loop(0, steps)
    def _(i):
        finish(1, i)

    @pl.loop(0, steps)
    def _(i):
        for h in range(2):
            for which in range(3):
                swap(h, which, i).wait_send()
            low(h, i).wait_send()
            deep(h, i).wait_send()
            store(h, i).wait()


def body(regions, fields, kriging, whitening, neighbours, home):
    blocks, points, order = kriging.shape
    series = fields.shape[1]
    region = 2 * blocks
    refs = neighbours.size
    steps = blocks // CHUNK
    any_space = pl.BlockSpec(memory_space=pl.ANY)
    smem = pl.BlockSpec(memory_space=pltpu.SMEM)
    dma = pltpu.SemaphoreType.DMA

    def rows(count):
        return pltpu.VMEM((count, points, series // 2), BF16)

    def halves(count):
        return pltpu.VMEM((2, count, points, series // 2), BF16)

    result = pl.pallas_call(
        functools.partial(kernel, regions),
        out_shape=jax.ShapeDtypeStruct((blocks, points, series), BF16),
        in_specs=[any_space, any_space, any_space, smem, smem],
        out_specs=any_space,
        scratch_shapes=[
            rows(3 * region), rows(3 * region),
            pltpu.VMEM((blocks, points, order), BF16),
            pltpu.VMEM((blocks, points, points), BF16),
            pltpu.VMEM((refs, points, points), BF16),
            pltpu.VMEM((blocks, points, points), BF16),
            rows(refs + 1), rows(refs + 1),
            halves(blocks),
            halves(3 * blocks),
            halves(2 * blocks),
            pltpu.SMEM((refs,), jnp.int32),
            pltpu.SMEM((3 * region,), jnp.int32),
            dma((4,)),
            dma((2 * steps,)), dma((2 * steps,)), dma((2 * steps,)), dma((2 * steps,)),
            dma((2,)), dma((2,)),
            dma((4 * steps,)), dma((4 * steps,)),
            dma((6 * steps,)), dma((6 * steps,)),
            dma((2 * steps,)), dma((2 * steps,)), dma((2 * steps,)), dma((2 * steps,)),
            dma((2 * steps,)),
        ],
        compiler_params=pltpu.CompilerParams(
            collective_id=0, has_side_effects=True, vmem_limit_bytes=56 * 1024 * 1024
        ),
        cost_estimate=pl.CostEstimate(
            flops=4 * blocks * points * series * (order + points),
            bytes_accessed=2 * (kriging.size + whitening.size + 2 * fields.size),
            transcendentals=0,
        ),
    )(fields.reshape(blocks, points, series), kriging, whitening, neighbours.T, home)
    return result.reshape(blocks * points, series)


def solution(mesh):
    return jax.shard_map(
        functools.partial(body, mesh.shape["space"]),
        mesh=mesh,
        in_specs=(
            P(("space", "sub"), None),
            P(("space", "sub"), None, None),
            P(("space", "sub"), None, None),
            P(("space", "sub"), None),
            P(),
        ),
        out_specs=P(("space", "sub"), None),
        check_vma=False,
    )
```

```python
import functools

import jax
import jax.numpy as jnp
from jax import lax
from jax.experimental import pallas as pl
from jax.experimental.pallas import tpu as pltpu
from jax.sharding import PartitionSpec as P

MESH = pl.DeviceIdType.MESH
F32 = jnp.float32
BF16 = jnp.bfloat16
CHUNK = 2
GROUP = 2
EARLY = 1


def kernel(
    regions,
    fields, kriging, whitening, neighbours, home,
    out,
    held_a, held_b, krig, white, krig_t, white_t, back_a, back_b, pulled, swapped, landed, places, inverse,
    load_sem, near_s, near_r, far_s, far_r, own_s, own_r, pass_s, pass_r,
    swap_s, swap_r, low_s, low_r, deep_s, deep_r, out_sem,
):
    held = (held_a, held_b)
    swapped = (swapped.at[0], swapped.at[1])
    landed = (landed.at[0], landed.at[1])
    pulled = (pulled.at[0], pulled.at[1])
    back = (back_a, back_b)
    blocks, points, series = fields.shape
    cols = series // 2
    region = 2 * blocks
    width = kriging.shape[2] // points
    refs = blocks * width
    steps = blocks // CHUNK
    half_steps = steps // 2
    me = lax.axis_index("space")
    core = lax.axis_index("sub")
    other = 1 - core
    parity = lax.rem(me, 2)
    even = parity == 0
    odd = parity == 1
    flip = me + 1 - 2 * parity
    ahead = lax.rem(me + 2, regions)
    behind = lax.rem(me + regions - 2, regions)
    partner = (me, other)
    mine = core * blocks
    theirs = other * blocks

    def send(src, dst, ssem, rsem, device):
        return pltpu.make_async_remote_copy(
            src_ref=src, dst_ref=dst, send_sem=ssem, recv_sem=rsem, device_id=device, device_id_type=MESH
        )

    def piece(ref, h, base, i):
        return ref[h].at[pl.ds(base + i * CHUNK, CHUNK)]

    def far(h, i):
        k = h * steps + i
        return send(
            piece(held, h, mine, i), piece(held, h, 2 * region + mine, i), far_s.at[k], far_r.at[k], (ahead, core)
        )

    def near(h, i, start):
        k = h * steps + i
        return send(
            piece(held, h, start + mine, i), piece(held, h, region + mine, i),
            near_s.at[k], near_r.at[k], (flip, core),
        )

    def own(h, half):
        spot = held[h].at[pl.ds(half, blocks)]
        return send(spot, spot, own_s.at[h], own_r.at[h], partner)

    def handed(h, which, half, i):
        spot = piece(held, h, which * region + half, i)
        k = (h * 2 + which - 1) * steps + i
        return send(spot, spot, pass_s.at[k], pass_r.at[k], partner)

    def load_fields(h):
        return pltpu.make_async_copy(
            fields.at[:, :, pl.ds(h * cols, cols)], held[h].at[pl.ds(mine, blocks)], load_sem.at[2 + h]
        )

    load_w = pltpu.make_async_copy(whitening, white, load_sem.at[0])
    load_k = pltpu.make_async_copy(kriging, krig, load_sem.at[1])
    load_fields(0).start()
    load_fields(1).start()
    load_w.start()
    load_k.start()

    barrier = pltpu.get_barrier_semaphore()
    for device in (partner, (flip, core), (ahead, core), (behind, core)):
        pl.semaphore_signal(barrier, inc=1, device_id=device, device_id_type=MESH)
    pl.semaphore_wait(barrier, 4)

    def start_own(h, i):
        far(h, i).start()

        @pl.when(even)
        def _():
            near(h, i, 0).start()

    load_fields(0).wait()

    @pl.loop(0, steps)
    def _(i):
        start_own(0, i)

    own(0, mine).start()
    load_fields(1).wait()
    own(1, mine).start()

    for h in range(2):
        back[h][refs] = jnp.zeros((points, cols), BF16)

    @pl.loop(0, blocks)
    def _(b):
        for k in range(width):
            slot = home[neighbours[k, b]]
            whose = slot // region
            distance = me - whose
            distance = jnp.where(distance < 0, distance + regions, distance)
            distance = jnp.minimum(distance, 2)
            places[b * width + k] = distance * region + slot - whose * region

    load_w.wait()
    load_k.wait()
    targets = 3 * region // steps

    def relay(h, i):
        far(h, i).wait_recv()

        @pl.when(odd)
        def _():
            near(h, i, 2 * region).start()

        handed(h, 2, mine, i).start()

    def relay_near(h, i):
        near(h, i, 0).wait_recv()
        handed(h, 1, mine, i).start()

    def arrived(h):
        own(h, theirs).wait_recv()

        @pl.loop(0, steps)
        def _(i):
            handed(h, 2, theirs, i).wait_recv()
            handed(h, 1, theirs, i).wait_recv()

    def sent(h):
        own(h, mine).wait_send()

        @pl.loop(0, steps)
        def _(i):
            far(h, i).wait_send()
            near(h, i, 0).wait_send()
            handed(h, 2, mine, i).wait_send()
            handed(h, 1, mine, i).wait_send()

    def dot(a, b):
        return jnp.dot(a, b, preferred_element_type=F32)

    def compute(h, g):
        group = [g * GROUP + d for d in range(GROUP)]
        preds = []
        for b in group:
            total = None
            for k in range(width):
                term = dot(krig[b, :, k * points : (k + 1) * points], held[h][places[b * width + k]])
                total = term if total is None else total + term
            preds.append(total)
        rests = [(held[h][mine + b].astype(F32) - p).astype(BF16) for b, p in zip(group, preds)]
        whites = [dot(white[b], r).astype(BF16) for b, r in zip(group, rests)]
        pulls = [dot(white_t[b], w).astype(BF16) for b, w in zip(group, whites)]
        for b, p in zip(group, pulls):
            pulled[h][b] = p
        for b, p in zip(group, pulls):
            for k in range(width):
                back[h][b * width + k] = dot(krig_t[b * width + k], p).astype(BF16)

    def swap(h, which, i):
        k = (h * 3 + which) * steps + i
        return send(
            piece(held, h, which * blocks, i), piece(swapped, h, which * blocks, i),
            swap_s.at[k], swap_r.at[k], partner,
        )

    def offer(h, which, i):
        for d in range(CHUNK):
            t = i * CHUNK + d
            held[h][which * blocks + t] = back[h][inverse[which * region + theirs + t]]
        swap(h, which, i).start()

    sums = 3 * blocks
    results = sums + 2 * blocks

    def low(h, i):
        k = h * steps + i
        return send(piece(held, h, sums, i), piece(landed, h, 0, i), low_s.at[k], low_r.at[k], (flip, core))

    def deep(h, i):
        k = h * steps + i
        return send(
            piece(held, h, sums + blocks, i), piece(landed, h, blocks, i), deep_s.at[k], deep_r.at[k], (behind, core)
        )

    def add_low(h, i):
        swap(h, 1, i).wait_recv()
        for d in range(CHUNK):
            t = i * CHUNK + d
            total = back[h][inverse[region + mine + t]].astype(F32) + swapped[h][blocks + t].astype(F32)
            held[h][sums + t] = total.astype(BF16)
        low(h, i).start()

    def add_deep(h, i, relayed):
        swap(h, 2, i).wait_recv()
        if relayed:
            low(h, i).wait_recv()
        for d in range(CHUNK):
            t = i * CHUNK + d
            total = back[h][inverse[2 * region + mine + t]].astype(F32) + swapped[h][2 * blocks + t].astype(F32)
            if relayed:
                total = total + landed[h][t].astype(F32)
            held[h][sums + blocks + t] = total.astype(BF16)
        deep(h, i).start()

    def add(h, i):
        add_low(h, i)

        @pl.when(even)
        def _():
            add_deep(h, i, False)

    def return_step(h, q):
        for e in range(2):
            offer(h, 1, 2 * q + e)
            offer(h, 2, 2 * q + e)

        @pl.when(q > 0)
        def _():
            for e in range(2):
                add(h, 2 * q - 2 + e)

    def return_end(h):
        for e in range(2):
            add(h, steps - 2 + e)

    def store(h, i):
        return pltpu.make_async_copy(
            piece(held, h, results, i),
            out.at[pl.ds(i * CHUNK, CHUNK), :, pl.ds(h * cols, cols)],
            out_sem.at[h * steps + i],
        )

    def finish(h, i):
        swap(h, 0, i).wait_recv()

        @pl.when(even)
        def _():
            low(h, i).wait_recv()

        deep(h, i).wait_recv()
        for d in range(CHUNK):
            t = i * CHUNK + d
            total = swapped[h][t].astype(F32) - pulled[h][t].astype(F32) + landed[h][blocks + t].astype(F32)
            total = total + jnp.where(even, landed[h][t].astype(F32), 0.0)
            held[h][results + t] = total.astype(BF16)
        store(h, i).start()

    @pl.loop(0, steps)
    def _(i):
        start_own(1, i)
        relay(0, i)

        for d in range(CHUNK):
            b = i * CHUNK + d
            white_t[b] = white[b].T
            for k in range(width):
                krig_t[b * width + k] = krig[b, :, k * points : (k + 1) * points].T

        @pl.loop(0, targets)
        def _(u):
            t = i * targets + u
            found = jnp.int32(refs)
            for j in range(refs):
                found = jnp.where(places[j] == t, j, found)
            inverse[t] = found

        relay_near(0, i)

    arrived(0)

    @pl.loop(0, half_steps)
    def _(q):
        relay(1, q)
        compute(0, 2 * q)
        relay_near(1, q)
        compute(0, 2 * q + 1)

    sent(0)

    @pl.loop(0, half_steps)
    def _(q):
        relay(1, q + half_steps)
        return_step(0, q)
        relay_near(1, q + half_steps)

    return_end(0)

    @pl.when(odd)
    def _():
        for j in range(EARLY):
            add_deep(0, j, True)

    arrived(1)

    @pl.loop(0, half_steps)
    def _(q):
        compute(1, 2 * q)
        compute(1, 2 * q + 1)

        @pl.when(odd)
        def _():
            add_deep(0, q + EARLY, True)

    sent(1)

    @pl.loop(0, half_steps)
    def _(q):
        return_step(1, q)

    return_end(1)

    @pl.when(odd)
    def _():
        @pl.loop(half_steps + EARLY, steps)
        def _(i):
            add_deep(0, i, True)

    @pl.loop(0, steps)
    def _(i):
        offer(0, 0, i)
        offer(1, 0, i)

    @pl.loop(0, steps)
    def _(i):
        @pl.when(odd)
        def _():
            add_deep(1, i, True)

        finish(0, i)

    @pl.loop(0, steps)
    def _(i):
        finish(1, i)

    @pl.loop(0, steps)
    def _(i):
        for h in range(2):
            for which in range(3):
                swap(h, which, i).wait_send()
            low(h, i).wait_send()
            deep(h, i).wait_send()
            store(h, i).wait()


def body(regions, fields, kriging, whitening, neighbours, home):
    blocks, points, order = kriging.shape
    series = fields.shape[1]
    region = 2 * blocks
    refs = neighbours.size
    steps = blocks // CHUNK
    any_space = pl.BlockSpec(memory_space=pl.ANY)
    smem = pl.BlockSpec(memory_space=pltpu.SMEM)
    dma = pltpu.SemaphoreType.DMA

    def rows(count):
        return pltpu.VMEM((count, points, series // 2), BF16)

    def halves(count):
        return pltpu.VMEM((2, count, points, series // 2), BF16)

    result = pl.pallas_call(
        functools.partial(kernel, regions),
        out_shape=jax.ShapeDtypeStruct((blocks, points, series), BF16),
        in_specs=[any_space, any_space, any_space, smem, smem],
        out_specs=any_space,
        scratch_shapes=[
            rows(3 * region), rows(3 * region),
            pltpu.VMEM((blocks, points, order), BF16),
            pltpu.VMEM((blocks, points, points), BF16),
            pltpu.VMEM((refs, points, points), BF16),
            pltpu.VMEM((blocks, points, points), BF16),
            rows(refs + 1), rows(refs + 1),
            halves(blocks),
            halves(3 * blocks),
            halves(2 * blocks),
            pltpu.SMEM((refs,), jnp.int32),
            pltpu.SMEM((3 * region,), jnp.int32),
            dma((4,)),
            dma((2 * steps,)), dma((2 * steps,)), dma((2 * steps,)), dma((2 * steps,)),
            dma((2,)), dma((2,)),
            dma((4 * steps,)), dma((4 * steps,)),
            dma((6 * steps,)), dma((6 * steps,)),
            dma((2 * steps,)), dma((2 * steps,)), dma((2 * steps,)), dma((2 * steps,)),
            dma((2 * steps,)),
        ],
        compiler_params=pltpu.CompilerParams(
            collective_id=0, has_side_effects=True, vmem_limit_bytes=56 * 1024 * 1024
        ),
        cost_estimate=pl.CostEstimate(
            flops=4 * blocks * points * series * (order + points),
            bytes_accessed=2 * (kriging.size + whitening.size + 2 * fields.size),
            transcendentals=0,
        ),
    )(fields.reshape(blocks, points, series), kriging, whitening, neighbours.T, home)
    return result.reshape(blocks * points, series)


def solution(mesh):
    return jax.shard_map(
        functools.partial(body, mesh.shape["space"]),
        mesh=mesh,
        in_specs=(
            P(("space", "sub"), None),
            P(("space", "sub"), None, None),
            P(("space", "sub"), None, None),
            P(("space", "sub"), None),
            P(),
        ),
        out_specs=P(("space", "sub"), None),
        check_vma=False,
    )
```

```python
import functools

import jax
import jax.numpy as jnp
from jax import lax
from jax.experimental import pallas as pl
from jax.experimental.pallas import tpu as pltpu
from jax.sharding import PartitionSpec as P

MESH = pl.DeviceIdType.MESH
F32 = jnp.float32
BF16 = jnp.bfloat16
CHUNK = 2
GROUP = 2
EARLY = 1


def kernel(
    regions,
    fields, kriging, whitening, neighbours, home,
    out,
    held_a, held_b, krig, white, krig_t, white_t, back_a, back_b, pulled, swapped, landed, places, inverse,
    load_sem, near_s, near_r, far_s, far_r, own_s, own_r, pass_s, pass_r,
    swap_s, swap_r, low_s, low_r, deep_s, deep_r, out_sem,
):
    held = (held_a, held_b)
    swapped = (swapped.at[0], swapped.at[1])
    landed = (landed.at[0], landed.at[1])
    pulled = (pulled.at[0], pulled.at[1])
    back = (back_a, back_b)
    blocks, points, series = fields.shape
    cols = series // 2
    region = 2 * blocks
    width = kriging.shape[2] // points
    refs = blocks * width
    steps = blocks // CHUNK
    half_steps = steps // 2
    me = lax.axis_index("space")
    core = lax.axis_index("sub")
    other = 1 - core
    parity = lax.rem(me, 2)
    even = parity == 0
    odd = parity == 1
    flip = me + 1 - 2 * parity
    ahead = lax.rem(me + 2, regions)
    behind = lax.rem(me + regions - 2, regions)
    partner = (me, other)
    mine = core * blocks
    theirs = other * blocks

    def send(src, dst, ssem, rsem, device):
        return pltpu.make_async_remote_copy(
            src_ref=src, dst_ref=dst, send_sem=ssem, recv_sem=rsem, device_id=device, device_id_type=MESH
        )

    def piece(ref, h, base, i):
        if i is None:
            return ref[h].at[pl.ds(base, blocks)]
        return ref[h].at[pl.ds(base + i * CHUNK, CHUNK)]

    def at(h, i):
        return h * steps + (0 if i is None else i)

    def far(h, i=None):
        k = at(h, i)
        return send(
            piece(held, h, mine, i), piece(held, h, 2 * region + mine, i), far_s.at[h], far_r.at[k], (ahead, core)
        )

    def near(h, i=None, start=0):
        k = at(h, i)
        return send(
            piece(held, h, start + mine, i), piece(held, h, region + mine, i),
            near_s.at[h], near_r.at[k], (flip, core),
        )

    def own(h, half):
        spot = held[h].at[pl.ds(half, blocks)]
        return send(spot, spot, own_s.at[h], own_r.at[h], partner)

    def handed(h, which, half, i=None):
        spot = piece(held, h, which * region + half, i)
        k = h * 2 + which - 1
        return send(spot, spot, pass_s.at[k], pass_r.at[k], partner)

    def load_fields(h):
        return pltpu.make_async_copy(
            fields.at[:, :, pl.ds(h * cols, cols)], held[h].at[pl.ds(mine, blocks)], load_sem.at[2 + h]
        )

    load_w = pltpu.make_async_copy(whitening, white, load_sem.at[0])
    load_k = pltpu.make_async_copy(kriging, krig, load_sem.at[1])
    load_fields(0).start()
    load_fields(1).start()
    load_w.start()
    load_k.start()

    barrier = pltpu.get_barrier_semaphore()
    for device in (partner, (flip, core), (ahead, core), (behind, core)):
        pl.semaphore_signal(barrier, inc=1, device_id=device, device_id_type=MESH)
    pl.semaphore_wait(barrier, 4)

    def start_own(h, i):
        far(h, i).start()

        @pl.when(even)
        def _():
            near(h, i, 0).start()

    load_fields(0).wait()

    @pl.loop(0, steps)
    def _(i):
        start_own(0, i)

    own(0, mine).start()
    load_fields(1).wait()
    own(1, mine).start()

    for h in range(2):
        back[h][refs] = jnp.zeros((points, cols), BF16)

    @pl.loop(0, blocks)
    def _(b):
        for k in range(width):
            slot = home[neighbours[k, b]]
            whose = slot // region
            distance = me - whose
            distance = jnp.where(distance < 0, distance + regions, distance)
            distance = jnp.minimum(distance, 2)
            places[b * width + k] = distance * region + slot - whose * region

    load_w.wait()
    load_k.wait()
    targets = 3 * region // steps

    def relay(h, i):
        far(h, i).wait_recv()

        @pl.when(odd)
        def _():
            near(h, i, 2 * region).start()

        handed(h, 2, mine, i).start()

    def relay_near(h, i):
        near(h, i, 0).wait_recv()
        handed(h, 1, mine, i).start()

    def arrived(h):
        own(h, theirs).wait_recv()
        handed(h, 2, theirs).wait_recv()
        handed(h, 1, theirs).wait_recv()

    def sent(h):
        own(h, mine).wait_send()
        far(h).wait_send()
        near(h).wait_send()
        handed(h, 2, mine).wait_send()
        handed(h, 1, mine).wait_send()

    def dot(a, b):
        return jnp.dot(a, b, preferred_element_type=F32)

    def compute(h, g):
        group = [g * GROUP + d for d in range(GROUP)]
        preds = []
        for b in group:
            total = None
            for k in range(width):
                term = dot(krig[b, :, k * points : (k + 1) * points], held[h][places[b * width + k]])
                total = term if total is None else total + term
            preds.append(total)
        rests = [(held[h][mine + b].astype(F32) - p).astype(BF16) for b, p in zip(group, preds)]
        whites = [dot(white[b], r).astype(BF16) for b, r in zip(group, rests)]
        pulls = [dot(white_t[b], w).astype(BF16) for b, w in zip(group, whites)]
        for b, p in zip(group, pulls):
            pulled[h][b] = p
        for b, p in zip(group, pulls):
            for k in range(width):
                back[h][b * width + k] = dot(krig_t[b * width + k], p).astype(BF16)

    def swap(h, which, i=None):
        k = (h * 3 + which) * steps + (0 if i is None else i)
        return send(
            piece(held, h, which * blocks, i), piece(swapped, h, which * blocks, i),
            swap_s.at[h * 3 + which], swap_r.at[k], partner,
        )

    def stage(h, which, i):
        for d in range(CHUNK):
            t = i * CHUNK + d
            held[h][which * blocks + t] = back[h][inverse[which * region + theirs + t]]

    def offer(h, which, i):
        stage(h, which, i)
        swap(h, which, i).start()

    sums = 3 * blocks
    results = sums + 2 * blocks

    def low(h, i=None):
        k = at(h, i)
        return send(piece(held, h, sums, i), piece(landed, h, 0, i), low_s.at[h], low_r.at[k], (flip, core))

    def deep(h, i=None):
        k = at(h, i)
        return send(
            piece(held, h, sums + blocks, i), piece(landed, h, blocks, i), deep_s.at[h], deep_r.at[k], (behind, core)
        )

    def add_low(h, i):
        swap(h, 1, i).wait_recv()
        for d in range(CHUNK):
            t = i * CHUNK + d
            total = back[h][inverse[region + mine + t]].astype(F32) + swapped[h][blocks + t].astype(F32)
            held[h][sums + t] = total.astype(BF16)
        low(h, i).start()

    def add_deep(h, i, relayed):
        swap(h, 2, i).wait_recv()
        if relayed:
            low(h, i).wait_recv()
        for d in range(CHUNK):
            t = i * CHUNK + d
            total = back[h][inverse[2 * region + mine + t]].astype(F32) + swapped[h][2 * blocks + t].astype(F32)
            if relayed:
                total = total + landed[h][t].astype(F32)
            held[h][sums + blocks + t] = total.astype(BF16)
        deep(h, i).start()

    def add(h, i):
        add_low(h, i)

        @pl.when(even)
        def _():
            add_deep(h, i, False)

    def return_step(h, q):
        for e in range(2):
            offer(h, 1, 2 * q + e)
            offer(h, 2, 2 * q + e)

        @pl.when(q > 0)
        def _():
            for e in range(2):
                add(h, 2 * q - 2 + e)

    def return_end(h):
        for e in range(2):
            add(h, steps - 2 + e)

    def store(h, i=None):
        spots = pl.ds(0, blocks) if i is None else pl.ds(i * CHUNK, CHUNK)
        return pltpu.make_async_copy(
            piece(held, h, results, i), out.at[spots, :, pl.ds(h * cols, cols)], out_sem.at[h]
        )

    def finish(h, i):
        @pl.when(even)
        def _():
            low(h, i).wait_recv()

        deep(h, i).wait_recv()
        for d in range(CHUNK):
            t = i * CHUNK + d
            total = swapped[h][t].astype(F32) - pulled[h][t].astype(F32) + landed[h][blocks + t].astype(F32)
            total = total + jnp.where(even, landed[h][t].astype(F32), 0.0)
            held[h][results + t] = total.astype(BF16)
        store(h, i).start()

    @pl.loop(0, steps)
    def _(i):
        start_own(1, i)
        relay(0, i)

        for d in range(CHUNK):
            b = i * CHUNK + d
            white_t[b] = white[b].T
            for k in range(width):
                krig_t[b * width + k] = krig[b, :, k * points : (k + 1) * points].T

        @pl.loop(0, targets)
        def _(u):
            t = i * targets + u
            found = jnp.int32(refs)
            for j in range(refs):
                found = jnp.where(places[j] == t, j, found)
            inverse[t] = found

        relay_near(0, i)

    arrived(0)

    @pl.loop(0, half_steps)
    def _(q):
        relay(1, q)
        compute(0, 2 * q)
        relay_near(1, q)
        compute(0, 2 * q + 1)

    sent(0)

    @pl.loop(0, half_steps)
    def _(q):
        relay(1, q + half_steps)
        return_step(0, q)
        relay_near(1, q + half_steps)

    return_end(0)

    @pl.when(odd)
    def _():
        for j in range(EARLY):
            add_deep(0, j, True)

    arrived(1)

    @pl.loop(0, half_steps)
    def _(q):
        compute(1, 2 * q)
        compute(1, 2 * q + 1)

        @pl.when(odd)
        def _():
            add_deep(0, q + EARLY, True)

    sent(1)

    @pl.loop(0, half_steps)
    def _(q):
        return_step(1, q)

    return_end(1)

    @pl.when(odd)
    def _():
        @pl.loop(half_steps + EARLY, steps)
        def _(i):
            add_deep(0, i, True)

    @pl.loop(0, steps)
    def _(i):
        stage(0, 0, i)
        stage(1, 0, i)

    swap(0, 0).start()
    swap(1, 0).start()
    swap(0, 0).wait_recv()

    @pl.loop(0, steps)
    def _(i):
        @pl.when(odd)
        def _():
            add_deep(1, i, True)

        finish(0, i)

    for which in range(3):
        swap(0, which).wait_send()
        swap(1, which).wait_send()
    swap(1, 0).wait_recv()
    low(0).wait_send()
    deep(0).wait_send()
    store(0).wait()

    @pl.loop(0, steps)
    def _(i):
        finish(1, i)

    low(1).wait_send()
    deep(1).wait_send()
    store(1).wait()


def body(regions, fields, kriging, whitening, neighbours, home):
    blocks, points, order = kriging.shape
    series = fields.shape[1]
    region = 2 * blocks
    refs = neighbours.size
    steps = blocks // CHUNK
    any_space = pl.BlockSpec(memory_space=pl.ANY)
    smem = pl.BlockSpec(memory_space=pltpu.SMEM)
    dma = pltpu.SemaphoreType.DMA

    def rows(count):
        return pltpu.VMEM((count, points, series // 2), BF16)

    def halves(count):
        return pltpu.VMEM((2, count, points, series // 2), BF16)

    result = pl.pallas_call(
        functools.partial(kernel, regions),
        out_shape=jax.ShapeDtypeStruct((blocks + 1, points, series), BF16),
        in_specs=[any_space, any_space, any_space, smem, smem],
        out_specs=any_space,
        scratch_shapes=[
            rows(3 * region), rows(3 * region),
            pltpu.VMEM((blocks, points, order), BF16),
            pltpu.VMEM((blocks, points, points), BF16),
            pltpu.VMEM((refs, points, points), BF16),
            pltpu.VMEM((blocks, points, points), BF16),
            rows(refs + 1), rows(refs + 1),
            halves(blocks),
            halves(3 * blocks),
            halves(2 * blocks),
            pltpu.SMEM((refs,), jnp.int32),
            pltpu.SMEM((3 * region,), jnp.int32),
            dma((4,)),
            dma((2,)), dma((2 * steps,)), dma((2,)), dma((2 * steps,)),
            dma((2,)), dma((2,)),
            dma((4,)), dma((4,)),
            dma((6,)), dma((6 * steps,)),
            dma((2,)), dma((2 * steps,)), dma((2,)), dma((2 * steps,)),
            dma((2,)),
        ],
        compiler_params=pltpu.CompilerParams(
            collective_id=0, has_side_effects=True, vmem_limit_bytes=56 * 1024 * 1024
        ),
        cost_estimate=pl.CostEstimate(
            flops=4 * blocks * points * series * (order + points),
            bytes_accessed=2 * (kriging.size + whitening.size + 2 * fields.size),
            transcendentals=0,
        ),
    )(fields.reshape(blocks, points, series), kriging, whitening, neighbours.T, home)
    return result[:blocks].reshape(blocks * points, series)


def solution(mesh):
    return jax.shard_map(
        functools.partial(body, mesh.shape["space"]),
        mesh=mesh,
        in_specs=(
            P(("space", "sub"), None),
            P(("space", "sub"), None, None),
            P(("space", "sub"), None, None),
            P(("space", "sub"), None),
            P(),
        ),
        out_specs=P(("space", "sub"), None),
        check_vma=False,
    )
```

```python
import functools

import jax
import jax.numpy as jnp
from jax import lax
from jax.experimental import pallas as pl
from jax.experimental.pallas import tpu as pltpu
from jax.sharding import PartitionSpec as P

MESH = pl.DeviceIdType.MESH
F32 = jnp.float32
BF16 = jnp.bfloat16
CHUNK = 2
OUTWARD = 1
GROUP = 2
EARLY = 1


def kernel(
    regions,
    fields, kriging, whitening, neighbours, home,
    out,
    held_a, held_b, krig, white, krig_t, white_t, back_a, back_b, pulled, swapped, landed, places, inverse,
    load_sem, near_s, near_r, far_s, far_r, own_s, own_r, pass_s, pass_r,
    swap_s, swap_r, low_s, low_r, deep_s, deep_r, out_sem,
):
    held = (held_a, held_b)
    swapped = (swapped.at[0], swapped.at[1])
    landed = (landed.at[0], landed.at[1])
    pulled = (pulled.at[0], pulled.at[1])
    back = (back_a, back_b)
    blocks, points, series = fields.shape
    cols = series // 2
    region = 2 * blocks
    width = kriging.shape[2] // points
    refs = blocks * width
    steps = blocks // CHUNK
    half_steps = steps // 2
    hops = blocks // OUTWARD
    quarter = hops // half_steps // 2
    me = lax.axis_index("space")
    core = lax.axis_index("sub")
    other = 1 - core
    parity = lax.rem(me, 2)
    even = parity == 0
    odd = parity == 1
    flip = me + 1 - 2 * parity
    ahead = lax.rem(me + 2, regions)
    behind = lax.rem(me + regions - 2, regions)
    partner = (me, other)
    mine = core * blocks
    theirs = other * blocks

    def send(src, dst, ssem, rsem, device):
        return pltpu.make_async_remote_copy(
            src_ref=src, dst_ref=dst, send_sem=ssem, recv_sem=rsem, device_id=device, device_id_type=MESH
        )

    def piece(ref, h, base, i):
        if i is None:
            return ref[h].at[pl.ds(base, blocks)]
        return ref[h].at[pl.ds(base + i * CHUNK, CHUNK)]

    def part(h, base, i):
        if i is None:
            return held[h].at[pl.ds(base, blocks)]
        return held[h].at[pl.ds(base + i * OUTWARD, OUTWARD)]

    def at(h, i):
        return h * steps + (0 if i is None else i)

    def hop(h, i):
        return h * hops + (0 if i is None else i)

    def far(h, i=None):
        k = hop(h, i)
        return send(
            part(h, mine, i), part(h, 2 * region + mine, i), far_s.at[h], far_r.at[k], (ahead, core)
        )

    def near(h, i=None, start=0):
        k = hop(h, i)
        return send(
            part(h, start + mine, i), part(h, region + mine, i),
            near_s.at[h], near_r.at[k], (flip, core),
        )

    def own(h, half):
        spot = held[h].at[pl.ds(half, blocks)]
        return send(spot, spot, own_s.at[h], own_r.at[h], partner)

    def handed(h, which, half, i=None):
        spot = part(h, which * region + half, i)
        k = h * 2 + which - 1
        return send(spot, spot, pass_s.at[k], pass_r.at[k], partner)

    def load_fields(h):
        return pltpu.make_async_copy(
            fields.at[:, :, pl.ds(h * cols, cols)], held[h].at[pl.ds(mine, blocks)], load_sem.at[2 + h]
        )

    load_w = pltpu.make_async_copy(whitening, white, load_sem.at[0])
    load_k = pltpu.make_async_copy(kriging, krig, load_sem.at[1])
    load_fields(0).start()
    load_fields(1).start()
    load_w.start()
    load_k.start()

    barrier = pltpu.get_barrier_semaphore()
    for device in (partner, (flip, core), (ahead, core), (behind, core)):
        pl.semaphore_signal(barrier, inc=1, device_id=device, device_id_type=MESH)
    pl.semaphore_wait(barrier, 4)

    def start_own(h, i):
        far(h, i).start()

        @pl.when(even)
        def _():
            near(h, i, 0).start()

    load_fields(0).wait()

    @pl.loop(0, hops)
    def _(i):
        start_own(0, i)

    own(0, mine).start()
    load_fields(1).wait()
    own(1, mine).start()

    for h in range(2):
        back[h][refs] = jnp.zeros((points, cols), BF16)

    @pl.loop(0, blocks)
    def _(b):
        for k in range(width):
            slot = home[neighbours[k, b]]
            whose = slot // region
            distance = me - whose
            distance = jnp.where(distance < 0, distance + regions, distance)
            distance = jnp.minimum(distance, 2)
            places[b * width + k] = distance * region + slot - whose * region

    load_w.wait()
    load_k.wait()
    targets = 3 * region // hops

    def relay(h, i):
        far(h, i).wait_recv()

        @pl.when(odd)
        def _():
            near(h, i, 2 * region).start()

        handed(h, 2, mine, i).start()

    def relay_near(h, i):
        near(h, i, 0).wait_recv()
        handed(h, 1, mine, i).start()

    def arrived(h):
        own(h, theirs).wait_recv()
        handed(h, 2, theirs).wait_recv()
        handed(h, 1, theirs).wait_recv()

    def sent(h):
        own(h, mine).wait_send()
        far(h).wait_send()
        near(h).wait_send()
        handed(h, 2, mine).wait_send()
        handed(h, 1, mine).wait_send()

    def dot(a, b):
        return jnp.dot(a, b, preferred_element_type=F32)

    def compute(h, g):
        group = [g * GROUP + d for d in range(GROUP)]
        preds = []
        for b in group:
            total = None
            for k in range(width):
                term = dot(krig[b, :, k * points : (k + 1) * points], held[h][places[b * width + k]])
                total = term if total is None else total + term
            preds.append(total)
        rests = [(held[h][mine + b].astype(F32) - p).astype(BF16) for b, p in zip(group, preds)]
        whites = [dot(white[b], r).astype(BF16) for b, r in zip(group, rests)]
        pulls = [dot(white_t[b], w).astype(BF16) for b, w in zip(group, whites)]
        for b, p in zip(group, pulls):
            pulled[h][b] = p
        for b, p in zip(group, pulls):
            for k in range(width):
                back[h][b * width + k] = dot(krig_t[b * width + k], p).astype(BF16)

    def swap(h, which, i=None):
        k = (h * 3 + which) * steps + (0 if i is None else i)
        return send(
            piece(held, h, which * blocks, i), piece(swapped, h, which * blocks, i),
            swap_s.at[h * 3 + which], swap_r.at[k], partner,
        )

    def stage(h, which, i):
        for d in range(CHUNK):
            t = i * CHUNK + d
            held[h][which * blocks + t] = back[h][inverse[which * region + theirs + t]]

    def offer(h, which, i):
        stage(h, which, i)
        swap(h, which, i).start()

    sums = 3 * blocks
    results = sums + 2 * blocks

    def low(h, i=None):
        k = at(h, i)
        return send(piece(held, h, sums, i), piece(landed, h, 0, i), low_s.at[h], low_r.at[k], (flip, core))

    def deep(h, i=None):
        k = at(h, i)
        return send(
            piece(held, h, sums + blocks, i), piece(landed, h, blocks, i), deep_s.at[h], deep_r.at[k], (behind, core)
        )

    def add_low(h, i):
        swap(h, 1, i).wait_recv()
        for d in range(CHUNK):
            t = i * CHUNK + d
            total = back[h][inverse[region + mine + t]].astype(F32) + swapped[h][blocks + t].astype(F32)
            held[h][sums + t] = total.astype(BF16)
        low(h, i).start()

    def add_deep(h, i, relayed):
        swap(h, 2, i).wait_recv()
        if relayed:
            low(h, i).wait_recv()
        for d in range(CHUNK):
            t = i * CHUNK + d
            total = back[h][inverse[2 * region + mine + t]].astype(F32) + swapped[h][2 * blocks + t].astype(F32)
            if relayed:
                total = total + landed[h][t].astype(F32)
            held[h][sums + blocks + t] = total.astype(BF16)
        deep(h, i).start()

    def add(h, i):
        add_low(h, i)

        @pl.when(even)
        def _():
            add_deep(h, i, False)

    def return_step(h, q):
        for e in range(2):
            offer(h, 1, 2 * q + e)
            offer(h, 2, 2 * q + e)

        @pl.when(q > 0)
        def _():
            for e in range(2):
                add(h, 2 * q - 2 + e)

    def return_end(h):
        for e in range(2):
            add(h, steps - 2 + e)

    def store(h, i=None):
        spots = pl.ds(0, blocks) if i is None else pl.ds(i * CHUNK, CHUNK)
        return pltpu.make_async_copy(
            piece(held, h, results, i), out.at[spots, :, pl.ds(h * cols, cols)], out_sem.at[h]
        )

    def finish(h, i):
        @pl.when(even)
        def _():
            low(h, i).wait_recv()

        deep(h, i).wait_recv()
        for d in range(CHUNK):
            t = i * CHUNK + d
            total = swapped[h][t].astype(F32) - pulled[h][t].astype(F32) + landed[h][blocks + t].astype(F32)
            total = total + jnp.where(even, landed[h][t].astype(F32), 0.0)
            held[h][results + t] = total.astype(BF16)
        store(h, i).start()

    @pl.loop(0, hops)
    def _(i):
        start_own(1, i)
        relay(0, i)

        for d in range(OUTWARD):
            b = i * OUTWARD + d
            white_t[b] = white[b].T
            for k in range(width):
                krig_t[b * width + k] = krig[b, :, k * points : (k + 1) * points].T

        @pl.loop(0, targets)
        def _(u):
            t = i * targets + u
            found = jnp.int32(refs)
            for j in range(refs):
                found = jnp.where(places[j] == t, j, found)
            inverse[t] = found

        relay_near(0, i)

    arrived(0)

    @pl.loop(0, half_steps)
    def _(q):
        for e in range(quarter):
            relay(1, q * quarter + e)
            compute(0, 2 * q + e)
            relay_near(1, q * quarter + e)

    sent(0)

    @pl.loop(0, half_steps)
    def _(q):
        for e in range(quarter):
            k = (half_steps + q) * quarter + e
            relay(1, k)
            if e == 0:
                return_step(0, q)
            relay_near(1, k)

    return_end(0)

    @pl.when(odd)
    def _():
        for j in range(EARLY):
            add_deep(0, j, True)

    arrived(1)

    @pl.loop(0, half_steps)
    def _(q):
        compute(1, 2 * q)
        compute(1, 2 * q + 1)

        @pl.when(odd)
        def _():
            add_deep(0, q + EARLY, True)

    sent(1)

    @pl.loop(0, half_steps)
    def _(q):
        return_step(1, q)

    return_end(1)

    @pl.when(odd)
    def _():
        @pl.loop(half_steps + EARLY, steps)
        def _(i):
            add_deep(0, i, True)

    @pl.loop(0, steps)
    def _(i):
        stage(0, 0, i)
        stage(1, 0, i)

    swap(0, 0).start()
    swap(1, 0).start()
    swap(0, 0).wait_recv()

    @pl.loop(0, steps)
    def _(i):
        @pl.when(odd)
        def _():
            add_deep(1, i, True)

        finish(0, i)

    for which in range(3):
        swap(0, which).wait_send()
        swap(1, which).wait_send()
    swap(1, 0).wait_recv()
    low(0).wait_send()
    deep(0).wait_send()
    store(0).wait()

    @pl.loop(0, steps)
    def _(i):
        finish(1, i)

    low(1).wait_send()
    deep(1).wait_send()
    store(1).wait()


def body(regions, fields, kriging, whitening, neighbours, home):
    blocks, points, order = kriging.shape
    series = fields.shape[1]
    region = 2 * blocks
    refs = neighbours.size
    steps = blocks // CHUNK
    hops = blocks // OUTWARD
    any_space = pl.BlockSpec(memory_space=pl.ANY)
    smem = pl.BlockSpec(memory_space=pltpu.SMEM)
    dma = pltpu.SemaphoreType.DMA

    def rows(count):
        return pltpu.VMEM((count, points, series // 2), BF16)

    def halves(count):
        return pltpu.VMEM((2, count, points, series // 2), BF16)

    result = pl.pallas_call(
        functools.partial(kernel, regions),
        out_shape=jax.ShapeDtypeStruct((blocks, points, series), BF16),
        in_specs=[any_space, any_space, any_space, smem, smem],
        out_specs=any_space,
        scratch_shapes=[
            rows(3 * region), rows(3 * region),
            pltpu.VMEM((blocks, points, order), BF16),
            pltpu.VMEM((blocks, points, points), BF16),
            pltpu.VMEM((refs, points, points), BF16),
            pltpu.VMEM((blocks, points, points), BF16),
            rows(refs + 1), rows(refs + 1),
            halves(blocks),
            halves(3 * blocks),
            halves(2 * blocks),
            pltpu.SMEM((refs,), jnp.int32),
            pltpu.SMEM((3 * region,), jnp.int32),
            dma((4,)),
            dma((2,)), dma((2 * hops,)), dma((2,)), dma((2 * hops,)),
            dma((2,)), dma((2,)),
            dma((4,)), dma((4,)),
            dma((6,)), dma((6 * steps,)),
            dma((2,)), dma((2 * steps,)), dma((2,)), dma((2 * steps,)),
            dma((2,)),
        ],
        compiler_params=pltpu.CompilerParams(
            collective_id=0, has_side_effects=True, vmem_limit_bytes=56 * 1024 * 1024
        ),
        cost_estimate=pl.CostEstimate(
            flops=4 * blocks * points * series * (order + points),
            bytes_accessed=2 * (kriging.size + whitening.size + 2 * fields.size),
            transcendentals=0,
        ),
    )(fields.reshape(blocks, points, series), kriging, whitening, neighbours.T, home)
    return result.reshape(blocks * points, series)


def solution(mesh):
    return jax.shard_map(
        functools.partial(body, mesh.shape["space"]),
        mesh=mesh,
        in_specs=(
            P(("space", "sub"), None),
            P(("space", "sub"), None, None),
            P(("space", "sub"), None, None),
            P(("space", "sub"), None),
            P(),
        ),
        out_specs=P(("space", "sub"), None),
        check_vma=False,
    )
```

```python
import functools

import jax
import jax.numpy as jnp
from jax import lax
from jax.experimental import pallas as pl
from jax.experimental.pallas import tpu as pltpu
from jax.sharding import PartitionSpec as P

MESH = pl.DeviceIdType.MESH
F32 = jnp.float32
BF16 = jnp.bfloat16
CHUNK = 2
OUTWARD = 1
GROUP = 2
EARLY = 1


def kernel(
    regions,
    fields, kriging, whitening, neighbours, home,
    out,
    held_a, held_b, krig, white, krig_t, white_t, back_a, back_b, pulled, swapped, landed, places, inverse,
    load_sem, near_s, near_r, far_s, far_r, own_s, own_r, pass_s, pass_r,
    swap_s, swap_r, low_s, low_r, deep_s, deep_r, out_sem,
):
    held = (held_a, held_b)
    swapped = (swapped.at[0], swapped.at[1])
    landed = (landed.at[0], landed.at[1])
    pulled = (pulled.at[0], pulled.at[1])
    back = (back_a, back_b)
    blocks, points, series = fields.shape
    cols = series // 2
    region = 2 * blocks
    width = kriging.shape[2] // points
    refs = blocks * width
    steps = blocks // CHUNK
    half_steps = steps // 2
    hops = blocks // OUTWARD
    quarter = hops // half_steps // 2
    me = lax.axis_index("space")
    core = lax.axis_index("sub")
    other = 1 - core
    parity = lax.rem(me, 2)
    even = parity == 0
    odd = parity == 1
    flip = me + 1 - 2 * parity
    ahead = lax.rem(me + 2, regions)
    behind = lax.rem(me + regions - 2, regions)
    partner = (me, other)
    mine = core * blocks
    theirs = other * blocks

    def send(src, dst, ssem, rsem, device):
        return pltpu.make_async_remote_copy(
            src_ref=src, dst_ref=dst, send_sem=ssem, recv_sem=rsem, device_id=device, device_id_type=MESH
        )

    def piece(ref, h, base, i):
        if i is None:
            return ref[h].at[pl.ds(base, blocks)]
        return ref[h].at[pl.ds(base + i * CHUNK, CHUNK)]

    def part(h, base, i):
        if i is None:
            return held[h].at[pl.ds(base, blocks)]
        return held[h].at[pl.ds(base + i * OUTWARD, OUTWARD)]

    def at(h, i):
        return h * steps + (0 if i is None else i)

    def hop(h, i):
        return h * hops + (0 if i is None else i)

    def far(h, i=None):
        k = hop(h, i)
        return send(
            part(h, mine, i), part(h, 2 * region + mine, i), far_s.at[h], far_r.at[k], (ahead, core)
        )

    def near(h, i=None, start=0):
        k = hop(h, i)
        return send(
            part(h, start + mine, i), part(h, region + mine, i),
            near_s.at[h], near_r.at[k], (flip, core),
        )

    def own(h, half):
        spot = held[h].at[pl.ds(half, blocks)]
        return send(spot, spot, own_s.at[h], own_r.at[h], partner)

    def handed(h, which, half, i=None):
        spot = part(h, which * region + half, i)
        k = h * 2 + which - 1
        return send(spot, spot, pass_s.at[k], pass_r.at[k], partner)

    def load_fields(h):
        return pltpu.make_async_copy(
            fields.at[:, :, pl.ds(h * cols, cols)], held[h].at[pl.ds(mine, blocks)], load_sem.at[2 + h]
        )

    load_w = pltpu.make_async_copy(whitening, white, load_sem.at[0])
    load_k = pltpu.make_async_copy(kriging, krig, load_sem.at[1])
    load_fields(0).start()
    load_fields(1).start()
    load_w.start()
    load_k.start()

    barrier = pltpu.get_barrier_semaphore()
    for device in (partner, (flip, core), (ahead, core), (behind, core)):
        pl.semaphore_signal(barrier, inc=1, device_id=device, device_id_type=MESH)
    pl.semaphore_wait(barrier, 4)

    def start_own(h, i):
        far(h, i).start()

        @pl.when(even)
        def _():
            near(h, i, 0).start()

    load_fields(0).wait()

    @pl.loop(0, hops)
    def _(i):
        start_own(0, i)

    own(0, mine).start()
    load_fields(1).wait()

    @pl.loop(0, hops)
    def _(i):
        start_own(1, i)

    own(1, mine).start()

    for h in range(2):
        back[h][refs] = jnp.zeros((points, cols), BF16)

    @pl.loop(0, blocks)
    def _(b):
        for k in range(width):
            slot = home[neighbours[k, b]]
            whose = slot // region
            distance = me - whose
            distance = jnp.where(distance < 0, distance + regions, distance)
            distance = jnp.minimum(distance, 2)
            places[b * width + k] = distance * region + slot - whose * region

    load_w.wait()
    load_k.wait()
    targets = 3 * region // hops

    def relay(h, i):
        far(h, i).wait_recv()

        @pl.when(odd)
        def _():
            near(h, i, 2 * region).start()

        handed(h, 2, mine, i).start()

    def relay_near(h, i):
        near(h, i, 0).wait_recv()
        handed(h, 1, mine, i).start()

    def arrived(h):
        own(h, theirs).wait_recv()
        handed(h, 2, theirs).wait_recv()
        handed(h, 1, theirs).wait_recv()

    def sent(h):
        own(h, mine).wait_send()
        far(h).wait_send()
        near(h).wait_send()
        handed(h, 2, mine).wait_send()
        handed(h, 1, mine).wait_send()

    def dot(a, b):
        return jnp.dot(a, b, preferred_element_type=F32)

    def compute(h, g):
        group = [g * GROUP + d for d in range(GROUP)]
        preds = []
        for b in group:
            total = None
            for k in range(width):
                term = dot(krig[b, :, k * points : (k + 1) * points], held[h][places[b * width + k]])
                total = term if total is None else total + term
            preds.append(total)
        rests = [(held[h][mine + b].astype(F32) - p).astype(BF16) for b, p in zip(group, preds)]
        whites = [dot(white[b], r).astype(BF16) for b, r in zip(group, rests)]
        pulls = [dot(white_t[b], w).astype(BF16) for b, w in zip(group, whites)]
        for b, p in zip(group, pulls):
            pulled[h][b] = p
        for b, p in zip(group, pulls):
            for k in range(width):
                back[h][b * width + k] = dot(krig_t[b * width + k], p).astype(BF16)

    def swap(h, which, i=None):
        k = (h * 3 + which) * steps + (0 if i is None else i)
        return send(
            piece(held, h, which * blocks, i), piece(swapped, h, which * blocks, i),
            swap_s.at[h * 3 + which], swap_r.at[k], partner,
        )

    def stage(h, which, i):
        for d in range(CHUNK):
            t = i * CHUNK + d
            held[h][which * blocks + t] = back[h][inverse[which * region + theirs + t]]

    def offer(h, which, i):
        stage(h, which, i)
        swap(h, which, i).start()

    sums = 3 * blocks
    results = sums + 2 * blocks

    def low(h, i=None):
        k = at(h, i)
        return send(piece(held, h, sums, i), piece(landed, h, 0, i), low_s.at[h], low_r.at[k], (flip, core))

    def deep(h, i=None):
        k = at(h, i)
        return send(
            piece(held, h, sums + blocks, i), piece(landed, h, blocks, i), deep_s.at[h], deep_r.at[k], (behind, core)
        )

    def add_low(h, i):
        swap(h, 1, i).wait_recv()
        for d in range(CHUNK):
            t = i * CHUNK + d
            total = back[h][inverse[region + mine + t]].astype(F32) + swapped[h][blocks + t].astype(F32)
            held[h][sums + t] = total.astype(BF16)
        low(h, i).start()

    def add_deep(h, i, relayed):
        swap(h, 2, i).wait_recv()
        if relayed:
            low(h, i).wait_recv()
        for d in range(CHUNK):
            t = i * CHUNK + d
            total = back[h][inverse[2 * region + mine + t]].astype(F32) + swapped[h][2 * blocks + t].astype(F32)
            if relayed:
                total = total + landed[h][t].astype(F32)
            held[h][sums + blocks + t] = total.astype(BF16)
        deep(h, i).start()

    def add(h, i):
        add_low(h, i)

        @pl.when(even)
        def _():
            add_deep(h, i, False)

    def return_step(h, q):
        for e in range(2):
            offer(h, 1, 2 * q + e)
            offer(h, 2, 2 * q + e)

        @pl.when(q > 0)
        def _():
            for e in range(2):
                add(h, 2 * q - 2 + e)

    def return_end(h):
        for e in range(2):
            add(h, steps - 2 + e)

    def store(h, i=None):
        spots = pl.ds(0, blocks) if i is None else pl.ds(i * CHUNK, CHUNK)
        return pltpu.make_async_copy(
            piece(held, h, results, i), out.at[spots, :, pl.ds(h * cols, cols)], out_sem.at[h]
        )

    def finish(h, i):
        @pl.when(even)
        def _():
            low(h, i).wait_recv()

        deep(h, i).wait_recv()
        for d in range(CHUNK):
            t = i * CHUNK + d
            total = swapped[h][t].astype(F32) - pulled[h][t].astype(F32) + landed[h][blocks + t].astype(F32)
            total = total + jnp.where(even, landed[h][t].astype(F32), 0.0)
            held[h][results + t] = total.astype(BF16)
        store(h, i).start()

    @pl.loop(0, hops)
    def _(i):
        relay(0, i)

        for d in range(OUTWARD):
            b = i * OUTWARD + d
            white_t[b] = white[b].T
            for k in range(width):
                krig_t[b * width + k] = krig[b, :, k * points : (k + 1) * points].T

        @pl.loop(0, targets)
        def _(u):
            t = i * targets + u
            found = jnp.int32(refs)
            for j in range(refs):
                found = jnp.where(places[j] == t, j, found)
            inverse[t] = found

        relay_near(0, i)

    arrived(0)

    @pl.loop(0, half_steps)
    def _(q):
        for e in range(quarter):
            relay(1, q * quarter + e)
            compute(0, 2 * q + e)
            relay_near(1, q * quarter + e)

    sent(0)

    @pl.loop(0, half_steps)
    def _(q):
        for e in range(quarter):
            k = (half_steps + q) * quarter + e
            relay(1, k)
            if e == 0:
                return_step(0, q)
            relay_near(1, k)

    return_end(0)

    @pl.when(odd)
    def _():
        for j in range(EARLY):
            add_deep(0, j, True)

    arrived(1)

    @pl.loop(0, half_steps)
    def _(q):
        compute(1, 2 * q)
        compute(1, 2 * q + 1)

        @pl.when(odd)
        def _():
            add_deep(0, q + EARLY, True)

    sent(1)

    @pl.loop(0, half_steps)
    def _(q):
        return_step(1, q)

    return_end(1)

    @pl.when(odd)
    def _():
        @pl.loop(half_steps + EARLY, steps)
        def _(i):
            add_deep(0, i, True)

    @pl.loop(0, steps)
    def _(i):
        stage(0, 0, i)
        stage(1, 0, i)

    swap(0, 0).start()
    swap(1, 0).start()
    swap(0, 0).wait_recv()

    @pl.loop(0, steps)
    def _(i):
        @pl.when(odd)
        def _():
            add_deep(1, i, True)

        finish(0, i)

    for which in range(3):
        swap(0, which).wait_send()
        swap(1, which).wait_send()
    swap(1, 0).wait_recv()
    low(0).wait_send()
    deep(0).wait_send()
    store(0).wait()

    @pl.loop(0, steps)
    def _(i):
        finish(1, i)

    low(1).wait_send()
    deep(1).wait_send()
    store(1).wait()


def body(regions, fields, kriging, whitening, neighbours, home):
    blocks, points, order = kriging.shape
    series = fields.shape[1]
    region = 2 * blocks
    refs = neighbours.size
    steps = blocks // CHUNK
    hops = blocks // OUTWARD
    any_space = pl.BlockSpec(memory_space=pl.ANY)
    smem = pl.BlockSpec(memory_space=pltpu.SMEM)
    dma = pltpu.SemaphoreType.DMA

    def rows(count):
        return pltpu.VMEM((count, points, series // 2), BF16)

    def halves(count):
        return pltpu.VMEM((2, count, points, series // 2), BF16)

    result = pl.pallas_call(
        functools.partial(kernel, regions),
        out_shape=jax.ShapeDtypeStruct((blocks, points, series), BF16),
        in_specs=[any_space, any_space, any_space, smem, smem],
        out_specs=any_space,
        scratch_shapes=[
            rows(3 * region), rows(3 * region),
            pltpu.VMEM((blocks, points, order), BF16),
            pltpu.VMEM((blocks, points, points), BF16),
            pltpu.VMEM((refs, points, points), BF16),
            pltpu.VMEM((blocks, points, points), BF16),
            rows(refs + 1), rows(refs + 1),
            halves(blocks),
            halves(3 * blocks),
            halves(2 * blocks),
            pltpu.SMEM((refs,), jnp.int32),
            pltpu.SMEM((3 * region,), jnp.int32),
            dma((4,)),
            dma((2,)), dma((2 * hops,)), dma((2,)), dma((2 * hops,)),
            dma((2,)), dma((2,)),
            dma((4,)), dma((4,)),
            dma((6,)), dma((6 * steps,)),
            dma((2,)), dma((2 * steps,)), dma((2,)), dma((2 * steps,)),
            dma((2,)),
        ],
        compiler_params=pltpu.CompilerParams(
            collective_id=0, has_side_effects=True, vmem_limit_bytes=56 * 1024 * 1024
        ),
        cost_estimate=pl.CostEstimate(
            flops=4 * blocks * points * series * (order + points),
            bytes_accessed=2 * (kriging.size + whitening.size + 2 * fields.size),
            transcendentals=0,
        ),
    )(fields.reshape(blocks, points, series), kriging, whitening, neighbours.T, home)
    return result.reshape(blocks * points, series)


def solution(mesh):
    return jax.shard_map(
        functools.partial(body, mesh.shape["space"]),
        mesh=mesh,
        in_specs=(
            P(("space", "sub"), None),
            P(("space", "sub"), None, None),
            P(("space", "sub"), None, None),
            P(("space", "sub"), None),
            P(),
        ),
        out_specs=P(("space", "sub"), None),
        check_vma=False,
    )
```
